256 devices in a mesh: date: 8 (over y, core), tile: 32 (over z, x).
Axes of the slice: x: 4, y: 4, z: 8, core: 2. Of those that a mesh axis runs over, the one named last changes fastest.
Arguments:
- granules: bfloat16 [32, 10, 2560, 512], P('date', None, 'tile'), may hold values from -6 to 6
- coef_x: bfloat16 [32, 5, 128, 12], P('tile'), may hold values from -1.75 to 1.75
- coef_y: bfloat16 [32, 5, 16, 12], P('tile'), may hold values from -1.75 to 1.75
- row_offset: int32 [32, 5], P('tile'), may hold values from 0 to 36
- col_offset: int32 [32, 5], P('tile'), may hold values from 0 to 244
- targets: int32 [32, 5], P('tile'), may hold values from -1 to 31, as said below
- mask: int32 [32, 32], P(None, 'tile'), may hold values from 0 to 1, as said below
- smoother: float32 [32, 32], replicated, as said below
Outputs:
- smoothed: float32 [32, 10, 32, 2048], P(None, None, 'tile', 'date')
The draws below stay inside these ranges and needn't reach their ends.
Inputs may be any that keep to these rules, and one draw needn't show every extreme that they name: `targets`: slot 0 of granule g names tile g; the other slots name, in an order drawn from the seed, each tile other than g within 2 of g in index once, and -1 where such a tile lies beyond the ends. `mask`: every tile has at least one valid date. `smoother`: every entry is positive.
All inputs are finite; a program needn't handle non-finite values.
Results may differ from the reference program's by a relative error of at most 0.0004.
Values sent between devices are 32-bit elements; how exact they have to be, the bound alone decides.
No kernel may reach another device: no remote copies, remote signals or barrier semaphores. Data moves between devices by JAX's collectives and lax.ppermute only.
A program may use at most 128 MiB of HBM per device.

```python
import jax
import jax.numpy as jnp
from jax import lax

BANDS = 10
TAPS = 12
RADIUS = 2
KMAX = 5
TR = 16
TC = 128
GR = 80
GC = 512
TILES = 32
DATES = 32


def draw_targets(key, part):
    key = jax.random.fold_in(key, 11)
    order_keys = jax.random.split(key, TILES)
    orders = jax.vmap(lambda single: jax.random.permutation(single, 2 * RADIUS))(order_keys)
    candidates = jnp.concatenate([jnp.arange(-RADIUS, 0, dtype=jnp.int32), jnp.arange(1, RADIUS + 1, dtype=jnp.int32)])
    reaches = candidates[orders]
    own_tile = jnp.arange(TILES, dtype=jnp.int32)[:, None]
    aimed = own_tile + reaches
    usable = (aimed >= 0) & (aimed < TILES)
    return jnp.concatenate([own_tile, jnp.where(usable, aimed, -1)], 1).astype(jnp.int32)


def draw_mask(key, part):
    key = jax.random.fold_in(key, 12)
    flag_key, pick_key = jax.random.split(key)
    flags = (jax.random.randint(flag_key, (DATES, TILES), 0, 10) < 7).astype(jnp.int32)
    picked = jax.random.randint(pick_key, (1, TILES), 0, DATES)
    forced = (jnp.arange(DATES, dtype=jnp.int32)[:, None] == picked).astype(jnp.int32)
    return jnp.maximum(flags, forced).astype(jnp.int32)


def draw_smoother(key, part):
    key = jax.random.fold_in(key, 13)
    places = jnp.arange(DATES, dtype=jnp.float32)
    gaps = jnp.abs(places[:, None] - places[None, :])
    decay = jnp.exp(-4.0 * gaps / DATES)
    factor = jax.random.uniform(key, (DATES, DATES), jnp.float32, 0.5, 1.5)
    return (decay * factor).astype(jnp.float32)


def plant(result, rng, low, high):
    index_at = [jax.random.randint(jax.random.fold_in(rng, axis), (), 0, length) for axis, length in enumerate(result.shape)]
    main_axis = result.shape.index(max(result.shape))
    next_to = index_at[:main_axis] + [(index_at[main_axis] + 1) % result.shape[main_axis]] + index_at[main_axis + 1:]
    return result.at[tuple(index_at)].set(low).at[tuple(next_to)].set(high)


def level_of(stream_key, extent, pieces, least, top_value):
    factor_of, own = 1.0, jax.random.fold_in(stream_key, 6)
    for position, parts in pieces:
        draws = jnp.exp(jax.random.uniform(jax.random.fold_in(own, position), (parts,), jnp.float32, least / len(pieces), top_value / len(pieces)))
        factor_of = factor_of * jnp.repeat(draws, extent[position] // parts).reshape([-1 if axis == position else 1 for axis in range(len(extent))])
    return factor_of


def bell_draw(key, shape, spread, bound, cuts=(), kind=jnp.bfloat16):
    factor_of = level_of(key, shape, cuts, -0.22, 0.18) if cuts else 1.0
    result = jax.random.normal(key, shape, jnp.float32) * spread * factor_of
    return jnp.minimum(jnp.maximum(result, -bound), bound).astype(kind)


def setup_inputs(seed: int = 0) -> dict:
    key_of = jax.random.split(jax.random.key(seed), 9)
    granules = bell_draw(key_of[0], (DATES, BANDS, TILES * GR, GC), 1.0, 6.0, ((0, 8), (2, 32)))
    coef_x = bell_draw(key_of[1], (TILES, KMAX, TC, TAPS), TAPS ** -0.5, 1.75, ((0, 32),))
    coef_y = bell_draw(key_of[2], (TILES, KMAX, TR, TAPS), TAPS ** -0.5, 1.75, ((0, 32),))
    row_offset = plant(jax.random.randint(key_of[3], (TILES, KMAX), 0, GR - 2 * TR - TAPS + 1), jax.random.fold_in(key_of[3], 1), 0, GR - 2 * TR - TAPS).astype(jnp.int32)
    col_offset = plant(jax.random.randint(key_of[4], (TILES, KMAX), 0, GC - 2 * TC - TAPS + 1), jax.random.fold_in(key_of[4], 1), 0, GC - 2 * TC - TAPS).astype(jnp.int32)
    targets = draw_targets(jax.random.fold_in(key_of[8], 71), 0)
    mask = draw_mask(jax.random.fold_in(key_of[8], 71), 0)
    smoother = draw_smoother(jax.random.fold_in(key_of[8], 71), 0)
    return dict(granules=granules, coef_x=coef_x, coef_y=coef_y, row_offset=row_offset, col_offset=col_offset, targets=targets, mask=mask, smoother=smoother)


def band_matrix(coeffs, offset, span_width):
    row_count = coeffs.shape[0]
    row_ids = jnp.arange(row_count, dtype=jnp.int32)[:, None]
    col_ids = jnp.arange(span_width, dtype=jnp.int32)[None, :]
    tap_index = col_ids - 2 * row_ids - offset.astype(jnp.int32)
    banded = jnp.zeros((row_count, span_width), jnp.float32)
    for tap_number in range(coeffs.shape[1]):
        picked = coeffs[:, tap_number:tap_number + 1].astype(jnp.float32)
        banded = banded + jnp.where(tap_index == tap_number, picked, jnp.float32(0.0))
    return banded


def resample(granule, x_coeffs, y_coeffs, row_shift, col_shift):
    slot_count = x_coeffs.shape[0]
    tile_cols = x_coeffs.shape[1]
    dates_here, band_count, grid_rows, grid_cols = granule.shape
    x_mats = jnp.concatenate([band_matrix(x_coeffs[slot], col_shift[slot], grid_cols) for slot in range(slot_count)], 0).astype(jnp.bfloat16)
    x_pass = jnp.dot(granule.reshape(-1, grid_cols), x_mats.T, preferred_element_type=jnp.float32)
    x_pass = x_pass.reshape(dates_here, band_count, grid_rows, slot_count, tile_cols)
    y_mats = jnp.stack([band_matrix(y_coeffs[slot], row_shift[slot], grid_rows) for slot in range(slot_count)], 0)
    return jnp.einsum("kir,dbrkj->kdbij", y_mats, x_pass, precision=lax.Precision.HIGHEST)


def reference(granules, coef_x, coef_y, row_offset, col_offset, targets, mask, smoother):
    def visit(tile_sums, inputs):
        granule_id, x_coeffs, y_coeffs, row_shift, col_shift, aimed = inputs
        granule = lax.dynamic_slice_in_dim(granules, granule_id * GR, GR, 2)
        partials = resample(granule, x_coeffs, y_coeffs, row_shift, col_shift)
        chosen = (aimed[:, None] == jnp.arange(TILES, dtype=jnp.int32)[None, :]).astype(jnp.float32)
        added = jnp.einsum("kt,kdbij->tdbij", chosen, partials, precision=lax.Precision.HIGHEST)
        return tile_sums + added, granule_id

    start_sums = jnp.zeros((TILES, DATES, BANDS, TR, TC), jnp.float32)
    tile_sums, ignored = lax.scan(visit, start_sums, (jnp.arange(TILES, dtype=jnp.int32), coef_x, coef_y, row_offset, col_offset, targets))
    series = tile_sums.reshape(TILES, DATES, BANDS, TR * TC)
    valid = mask.astype(jnp.float32)
    weighted = series * jnp.transpose(valid)[:, :, None, None]
    numerator = jnp.einsum("ts,usbp->tbup", smoother, weighted, precision=lax.Precision.HIGHEST)
    denominator = jnp.dot(smoother, valid, precision=lax.Precision.HIGHEST)
    return numerator / denominator[:, None, :, None]
```

```python
import functools

import jax
import jax.numpy as jnp
from jax import lax
from jax.experimental import pallas as pl
from jax.experimental.pallas import tpu as pltpu
from jax.sharding import PartitionSpec as P

HIGHEST = lax.Precision.HIGHEST


def even_swap(block):
    pairs = [(i, i ^ 1) for i in range(lax.axis_size("tile"))]
    return lax.ppermute(block, "tile", pairs)


def odd_swap(block):
    last = lax.axis_size("tile") - 1
    pairs = [(i, i if i in (0, last) else ((i - 1) ^ 1) + 1) for i in range(last + 1)]
    return lax.ppermute(block, "tile", pairs)


def resample_kernel(reaches, targets, row_offset, col_offset, coef_x, coef_y, granule, *rest):
    count = len(reaches)
    outs, (x_mats, y_mats) = rest[:count], rest[count:]
    slots = coef_x.shape[1]
    tile_cols, taps = coef_x.shape[2:]
    tile_rows = coef_y.shape[2]
    bands, grid_rows, grid_cols = granule.shape[1:]
    date = pl.program_id(0)

    @pl.when(date == 0)
    def build():
        own = lax.axis_index("tile")
        side = 1 - 2 * lax.rem(own, 2)
        to_order = (
            lax.broadcasted_iota(jnp.int32, (tile_rows, tile_rows), 1)
            == 2 * lax.rem(lax.broadcasted_iota(jnp.int32, (tile_rows, tile_rows), 0), tile_rows // 2)
            + lax.broadcasted_iota(jnp.int32, (tile_rows, tile_rows), 0) // (tile_rows // 2)
        ).astype(jnp.float32)
        for n, reach in enumerate(reaches):
            wanted = own + side * reach
            slot = jnp.int32(0)
            used = jnp.int32(0)
            for k in range(slots):
                hit = jnp.logical_and(wanted >= 0, targets[0, k] == wanted).astype(jnp.int32)
                slot = slot + k * hit
                used = used + hit
            tap = (
                lax.broadcasted_iota(jnp.int32, (tile_cols, grid_cols), 1)
                - 2 * lax.broadcasted_iota(jnp.int32, (tile_cols, grid_cols), 0)
                - col_offset[0, slot]
            )
            coeffs = coef_x[0, slot].astype(jnp.float32)
            banded = jnp.zeros((tile_cols, grid_cols), jnp.float32)
            for t in range(taps):
                banded = jnp.where(tap == t, coeffs[:, t : t + 1], banded)
            x_mats[n] = banded.astype(jnp.bfloat16)
            tap = (
                lax.broadcasted_iota(jnp.int32, (tile_rows, grid_rows), 1)
                - 2 * lax.broadcasted_iota(jnp.int32, (tile_rows, grid_rows), 0)
                - row_offset[0, slot]
            )
            tap = jnp.where(used > 0, tap, -1)
            coeffs = coef_y[0, slot].astype(jnp.float32)
            banded = jnp.zeros((tile_rows, grid_rows), jnp.float32)
            for t in range(taps):
                banded = jnp.where(tap == t, coeffs[:, t : t + 1], banded)
            ordered = jnp.dot(to_order, banded, preferred_element_type=jnp.float32)
            y_mats[n * tile_rows : (n + 1) * tile_rows] = ordered.astype(jnp.bfloat16)

    along_y = [
        jnp.dot(y_mats[...], granule[0, b], preferred_element_type=jnp.float32) for b in range(bands)
    ]
    half = tile_rows // 2
    for n in range(count):
        rows = jnp.concatenate([part[n * tile_rows : (n + 1) * tile_rows] for part in along_y], 0)
        high = rows.astype(jnp.bfloat16)
        low = (rows - high.astype(jnp.float32)).astype(jnp.bfloat16)
        both = lax.dot_general(
            jnp.concatenate([high, low], 0),
            x_mats[n],
            (((1,), (1,)), ((), ())),
            preferred_element_type=jnp.float32,
        )
        partial = both[: bands * tile_rows] + both[bands * tile_rows :]
        stride = outs[n].shape[0] // half
        for b in range(bands):
            for parity in range(2):
                first = b * tile_rows + parity * half
                outs[n][pl.ds(date * 2 * bands + parity * bands + b, half, stride=stride), :] = partial[
                    first : first + half
                ]


def resample(reaches, chunk, chunks, targets, row_offset, col_offset, coef_x, coef_y, granules):
    dates, bands, grid_rows, grid_cols = granules.shape
    slots, tile_cols = coef_x.shape[1:3]
    tile_rows = coef_y.shape[2]
    bands = bands // chunks
    rows = dates * bands * tile_rows
    count = len(reaches)
    smem = pl.BlockSpec(memory_space=pltpu.SMEM)
    return pl.pallas_call(
        functools.partial(resample_kernel, reaches),
        grid=(dates,),
        in_specs=[
            smem,
            smem,
            smem,
            pl.BlockSpec(coef_x.shape, lambda d: (0, 0, 0, 0)),
            pl.BlockSpec(coef_y.shape, lambda d: (0, 0, 0, 0)),
            pl.BlockSpec((1, bands, grid_rows, grid_cols), lambda d: (d, chunk, 0, 0)),
        ],
        out_specs=[pl.BlockSpec((rows, tile_cols), lambda d: (0, 0))] * count,
        out_shape=[jax.ShapeDtypeStruct((rows, tile_cols), jnp.float32)] * count,
        scratch_shapes=[
            pltpu.VMEM((count, tile_cols, grid_cols), jnp.bfloat16),
            pltpu.VMEM((count * tile_rows, grid_rows), jnp.bfloat16),
        ],
        compiler_params=pltpu.CompilerParams(vmem_limit_bytes=32 * 1024 * 1024),
        cost_estimate=pl.CostEstimate(
            flops=count * dates * bands * tile_rows * grid_cols * (grid_rows + 4 * tile_cols),
            bytes_accessed=granules.size * 2 // chunks,
            transcendentals=0,
        ),
        name="resample",
    )(targets, row_offset, col_offset, coef_x, coef_y, granules)


def smooth_kernel(parts, mask, smoother, *refs):
    series, out = refs[:-1], refs[-1]
    dates = smoother.shape[0]
    lanes = out.shape[1]
    weight = jnp.broadcast_to(mask[...].astype(jnp.float32), (dates, lanes))
    weights = smoother[...]
    denominator = jnp.dot(weights, weight, precision=HIGHEST, preferred_element_type=jnp.float32)
    stride = out.shape[0] // dates
    bands = series[0].shape[0] // dates // 2
    for c in range(parts):
        for b in range(bands):
            for parity in range(2):
                picked = series[c][pl.ds(parity * bands + b, dates, stride=2 * bands), :]
                total = jnp.dot(
                    weights, picked * weight, precision=HIGHEST, preferred_element_type=jnp.float32
                )
                out[pl.ds(2 * (c * bands + b) + parity, dates, stride=stride), :] = total / denominator


def smooth(mask, smoother, series):
    rows = sum(part.shape[0] for part in series)
    lanes = series[0].shape[1]
    return pl.pallas_call(
        functools.partial(smooth_kernel, len(series)),
        out_shape=jax.ShapeDtypeStruct((rows, lanes), jnp.float32),
        compiler_params=pltpu.CompilerParams(vmem_limit_bytes=32 * 1024 * 1024),
        name="smooth",
    )(mask, smoother, *series)


def to_pixel_blocks(part):
    return lax.all_to_all(part, "date", split_axis=0, concat_axis=0, tiled=True)


CHUNKS = 1


def body(granules, coef_x, coef_y, row_offset, col_offset, targets, mask, smoother):
    bands = granules.shape[1]
    block_pix = coef_x.shape[2] * coef_y.shape[2] // lax.axis_size("date")

    def run(reaches, chunk):
        return resample(
            reaches, chunk, CHUNKS, targets, row_offset, col_offset, coef_x, coef_y, granules
        )

    far = [run((2, -2), c) for c in range(CHUNKS)]
    passed = [(even_swap(even), odd_swap(odd)) for even, odd in far]
    near = [run((1, -1, 0), c) for c in range(CHUNKS)]
    arrived = [
        (even_swap(even + from_odd), odd_swap(odd + from_even))
        for (even, odd, _), (from_even, from_odd) in zip(near, passed)
    ]
    series = [own + even + odd for (_, _, own), (even, odd) in zip(near, arrived)]
    blocks = [to_pixel_blocks(part) for part in series]
    smoothed = smooth(mask, smoother, blocks)
    return smoothed.reshape(smoother.shape[0], bands, 1, block_pix)


def solution(mesh):
    return jax.shard_map(
        body,
        mesh=mesh,
        in_specs=(
            P("date", None, "tile", None),
            P("tile", None, None, None),
            P("tile", None, None, None),
            P("tile", None),
            P("tile", None),
            P("tile", None),
            P(None, "tile"),
            P(),
        ),
        out_specs=P(None, None, "tile", "date"),
        check_vma=False,
    )
```

```python
import functools

import jax
import jax.numpy as jnp
from jax import lax
from jax.experimental import pallas as pl
from jax.experimental.pallas import tpu as pltpu
from jax.sharding import PartitionSpec as P

HIGHEST = lax.Precision.HIGHEST
CHUNKS = (10,)


def even_swap(block):
    pairs = [(i, i ^ 1) for i in range(lax.axis_size("tile"))]
    return lax.ppermute(block, "tile", pairs)


def odd_swap(block):
    tiles = lax.axis_size("tile")
    pairs = []
    for date in range(lax.axis_size("date")):
        for tile in range(tiles):
            other, date_to = ((tile - 1) ^ 1) + 1, date
            if tile in (0, tiles - 1):
                other, date_to = tile, date ^ 1
            pairs.append((date * tiles + tile, date_to * tiles + other))
    return lax.ppermute(block, ("date", "tile"), pairs)


def date_swap(block, distance):
    return lax.ppermute(block, "date", [(i, i ^ distance) for i in range(lax.axis_size("date"))])


def resample_kernel(reaches, *refs):
    count = len(reaches)
    parts = count * len(CHUNKS)
    inputs, outs, scratch = refs[:6], refs[6 : 6 + parts], refs[6 + parts :]
    held, (x_mats, y_mats, sems, date_sems) = scratch[:6], scratch[6:]
    targets, row_offset, col_offset, coef_x, coef_y, granule = held
    slots, taps, tile_cols = coef_x.shape[1:]
    tile_rows = coef_y.shape[2]
    dates, bands, grid_rows, grid_cols = granule.shape

    small = [pltpu.make_async_copy(inputs[i], held[i], sems.at[i]) for i in range(5)]
    large = [
        pltpu.make_async_copy(inputs[5].at[d], granule.at[d], date_sems.at[d])
        for d in range(dates)
    ]
    for copy in small + large:
        copy.start()
    for copy in small:
        copy.wait()

    own = lax.axis_index("tile")
    side = 1 - 2 * lax.rem(own, 2)
    to_order = (
        lax.broadcasted_iota(jnp.int32, (tile_rows, tile_rows), 1)
        == 2 * lax.rem(lax.broadcasted_iota(jnp.int32, (tile_rows, tile_rows), 0), tile_rows // 2)
        + lax.broadcasted_iota(jnp.int32, (tile_rows, tile_rows), 0) // (tile_rows // 2)
    ).astype(jnp.float32)
    for n, reach in enumerate(reaches):
        wanted = own + side * reach
        slot = jnp.int32(0)
        used = jnp.int32(0)
        for k in range(slots):
            hit = jnp.logical_and(wanted >= 0, targets[0, k] == wanted).astype(jnp.int32)
            slot = slot + k * hit
            used = used + hit
        tap = (
            lax.broadcasted_iota(jnp.int32, (grid_cols, tile_cols), 0)
            - 2 * lax.broadcasted_iota(jnp.int32, (grid_cols, tile_cols), 1)
            - col_offset[0, slot]
        )
        coeffs = coef_x[0, slot].astype(jnp.float32)
        banded = jnp.zeros((grid_cols, tile_cols), jnp.float32)
        for t in range(taps):
            banded = jnp.where(tap == t, coeffs[t : t + 1, :], banded)
        x_mats[n] = banded.astype(jnp.bfloat16)
        tap = (
            lax.broadcasted_iota(jnp.int32, (tile_rows, grid_rows), 1)
            - 2 * lax.broadcasted_iota(jnp.int32, (tile_rows, grid_rows), 0)
            - row_offset[0, slot]
        )
        tap = jnp.where(used > 0, tap, -1)
        coeffs = coef_y[0, slot].astype(jnp.float32)
        banded = jnp.zeros((tile_rows, grid_rows), jnp.float32)
        for t in range(taps):
            banded = jnp.where(tap == t, coeffs[:, t : t + 1], banded)
        ordered = jnp.dot(to_order, banded, preferred_element_type=jnp.float32)
        y_mats[n * tile_rows : (n + 1) * tile_rows] = ordered.astype(jnp.bfloat16)

    half = tile_rows // 2
    for date in range(dates):
        large[date].wait()
        along_y = [
            jnp.dot(y_mats[...], granule[date, b], preferred_element_type=jnp.float32)
            for b in range(bands)
        ]
        for n in range(count):
            rows = jnp.concatenate([part[n * tile_rows : (n + 1) * tile_rows] for part in along_y], 0)
            high = rows.astype(jnp.bfloat16)
            low = (rows - high.astype(jnp.float32)).astype(jnp.bfloat16)
            both = jnp.dot(
                jnp.concatenate([high, low], 0), x_mats[n], preferred_element_type=jnp.float32
            )
            partial = both[: bands * tile_rows] + both[bands * tile_rows :]
            start = 0
            for c, width in enumerate(CHUNKS):
                out = outs[n * len(CHUNKS) + c]
                stride = out.shape[0] // half
                for b in range(width):
                    for parity in range(2):
                        first = (start + b) * tile_rows + parity * half
                        at = date * 2 * width + parity * width + b
                        out[pl.ds(at, half, stride=stride), :] = partial[first : first + half]
                start += width


def resample(reaches, limit, targets, row_offset, col_offset, coef_x, coef_y, granules):
    dates, bands, grid_rows, grid_cols = granules.shape
    taps, tile_cols = coef_x.shape[2:]
    tile_rows = coef_y.shape[2]
    count = len(reaches)
    shapes = [
        jax.ShapeDtypeStruct((dates * width * tile_rows, tile_cols), jnp.float32) for width in CHUNKS
    ] * count
    outs = pl.pallas_call(
        functools.partial(resample_kernel, reaches),
        in_specs=[pl.BlockSpec(memory_space=pltpu.HBM)] * 6,
        out_specs=[pl.BlockSpec(memory_space=pltpu.VMEM)] * len(shapes),
        out_shape=shapes,
        scratch_shapes=[
            pltpu.SMEM(targets.shape, jnp.int32),
            pltpu.SMEM(row_offset.shape, jnp.int32),
            pltpu.SMEM(col_offset.shape, jnp.int32),
            pltpu.VMEM(coef_x.shape, coef_x.dtype),
            pltpu.VMEM(coef_y.shape, coef_y.dtype),
            pltpu.VMEM((dates, bands, grid_rows, grid_cols), granules.dtype),
            pltpu.VMEM((count, grid_cols, tile_cols), jnp.bfloat16),
            pltpu.VMEM((count * tile_rows, grid_rows), jnp.bfloat16),
            pltpu.SemaphoreType.DMA((5,)),
            pltpu.SemaphoreType.DMA((dates,)),
        ],
        compiler_params=pltpu.CompilerParams(vmem_limit_bytes=limit),
        cost_estimate=pl.CostEstimate(
            flops=count * dates * bands * tile_rows * grid_cols * (grid_rows + 4 * tile_cols),
            bytes_accessed=granules.size * 2,
            transcendentals=0,
        ),
        name="resample",
    )(targets, row_offset, col_offset, coef_x, coef_y, granules)
    return [outs[c :: len(CHUNKS)] for c in range(len(CHUNKS))]


def weights_kernel(local_dates, mask, smoother, weights, totals):
    dates = smoother.shape[0]
    masked = smoother[...] * mask[...].astype(jnp.float32)
    me = lax.axis_index("date")
    source = lax.broadcasted_iota(jnp.int32, (dates, dates), 0)
    place = lax.broadcasted_iota(jnp.int32, (dates, dates), 1)
    wanted = ((place // local_dates) ^ me) * local_dates + lax.rem(place, local_dates)
    picks = (source == wanted).astype(jnp.float32)
    weights[...] = jnp.dot(masked, picks, precision=HIGHEST, preferred_element_type=jnp.float32)
    totals[...] = jnp.broadcast_to(jnp.sum(masked, 1, keepdims=True), totals.shape)


def smoothing_weights(local_dates, lanes, mask, smoother):
    return pl.pallas_call(
        functools.partial(weights_kernel, local_dates),
        out_shape=[
            jax.ShapeDtypeStruct(smoother.shape, jnp.float32),
            jax.ShapeDtypeStruct((smoother.shape[0], lanes), jnp.float32),
        ],
        compiler_params=pltpu.CompilerParams(vmem_limit_bytes=32 * 1024 * 1024),
        name="smoothing_weights",
    )(mask, smoother)


def smooth_kernel(pieces, weights, totals, *refs):
    series, out = refs[:-1], refs[-1]
    dates = weights.shape[0]
    stride = out.shape[0] // dates
    held = dates // pieces
    start = 0
    for c, bands in enumerate(CHUNKS):
        for b in range(bands):
            for parity in range(2):
                picked = jnp.concatenate(
                    [
                        part[pl.ds(parity * bands + b, held, stride=2 * bands), :]
                        for part in series[c * pieces : (c + 1) * pieces]
                    ],
                    0,
                )
                total = jnp.dot(
                    weights[...], picked, precision=HIGHEST, preferred_element_type=jnp.float32
                )
                at = 2 * (start + b) + parity
                out[pl.ds(at, dates, stride=stride), :] = total / totals[...]
        start += bands


def smooth(weights, totals, series):
    return pl.pallas_call(
        functools.partial(smooth_kernel, len(series[0])),
        out_shape=jax.ShapeDtypeStruct(
            (sum(part.shape[0] for chunk in series for part in chunk), totals.shape[1]), jnp.float32
        ),
        compiler_params=pltpu.CompilerParams(vmem_limit_bytes=32 * 1024 * 1024),
        name="smooth",
    )(weights, totals, *[part for chunk in series for part in chunk])


def to_pixel_blocks(terms):
    positions = lax.axis_size("date")
    me = lax.axis_index("date")
    core, y = lax.rem(me, 2), me // 2
    terms = [term.reshape(positions // 2, 2, -1, term.shape[-1]) for term in terms]

    def of_core(which):
        picked = [lax.dynamic_index_in_dim(term, which, 1, keepdims=False) for term in terms]
        return picked[0] + picked[1] + picked[2]

    mine, other = of_core(core), of_core(1 - core)
    got = date_swap(other, 1)
    blocks = []
    for distance in range(positions // 2):
        at = y ^ distance
        block = jnp.concatenate(
            [
                lax.dynamic_index_in_dim(mine, at, 0, keepdims=False),
                lax.dynamic_index_in_dim(got, at, 0, keepdims=False),
            ],
            0,
        )
        blocks.append(date_swap(block, 2 * distance) if distance else block)
    return blocks


def body(granules, coef_x, coef_y, row_offset, col_offset, targets, mask, smoother):
    local_dates, bands = granules.shape[:2]
    tile_cols = coef_x.shape[2]
    block_pix = tile_cols * coef_y.shape[2] // lax.axis_size("date")
    coef_x = jnp.transpose(coef_x, (0, 1, 3, 2))

    def run(reaches, limit):
        return resample(reaches, limit, targets, row_offset, col_offset, coef_x, coef_y, granules)

    weights, totals = smoothing_weights(local_dates, tile_cols, jnp.transpose(mask), smoother)
    far = run((2, -2), None)
    passed = [(even_swap(even), odd_swap(odd)) for even, odd in far]
    near = run((1, -1, 0), 32 * 1024 * 1024)
    arrived = [
        (even_swap(even + from_odd), odd_swap(odd + from_even))
        for (even, odd, _), (from_even, from_odd) in zip(near, passed)
    ]
    blocks = [to_pixel_blocks((own, even, odd)) for (_, _, own), (even, odd) in zip(near, arrived)]
    smoothed = smooth(weights, totals, blocks)
    return smoothed.reshape(smoother.shape[0], bands, 1, block_pix)


def solution(mesh):
    return jax.shard_map(
        body,
        mesh=mesh,
        in_specs=(
            P("date", None, "tile", None),
            P("tile", None, None, None),
            P("tile", None, None, None),
            P("tile", None),
            P("tile", None),
            P("tile", None),
            P(None, "tile"),
            P(),
        ),
        out_specs=P(None, None, "tile", "date"),
        check_vma=False,
    )
```

```python
import functools

import jax
import jax.numpy as jnp
from jax import lax
from jax.experimental import pallas as pl
from jax.experimental.pallas import tpu as pltpu
from jax.sharding import PartitionSpec as P

HIGHEST = lax.Precision.HIGHEST
CHUNKS = (10,)
LIMIT = 12 * 1024 * 1024


def even_swap(block):
    pairs = [(i, i ^ 1) for i in range(lax.axis_size("tile"))]
    return lax.ppermute(block, "tile", pairs)


def odd_swap(block):
    tiles = lax.axis_size("tile")
    pairs = []
    for date in range(lax.axis_size("date")):
        for tile in range(tiles):
            other, date_to = ((tile - 1) ^ 1) + 1, date
            if tile in (0, tiles - 1):
                other, date_to = tile, date ^ 1
            pairs.append((date * tiles + tile, date_to * tiles + other))
    return lax.ppermute(block, ("date", "tile"), pairs)


def date_swap(block, distance):
    return lax.ppermute(block, "date", [(i, i ^ distance) for i in range(lax.axis_size("date"))])


def resample_kernel(reaches, extra, *refs):
    count = len(reaches)
    parts = count * len(CHUNKS)
    inputs, refs = refs[:6], refs[6 + extra :]
    outs, scratch = refs[:parts], refs[parts + extra // 2 :]
    held, (x_mats, y_mats, sems, date_sems) = scratch[:6], scratch[6:]
    targets, row_offset, col_offset, coef_x, coef_y, granule = held
    slots, taps, tile_cols = coef_x.shape[1:]
    tile_rows = coef_y.shape[2]
    dates, bands, grid_rows, grid_cols = granule.shape

    small = [pltpu.make_async_copy(inputs[i], held[i], sems.at[i]) for i in range(5)]
    large = [
        pltpu.make_async_copy(inputs[5].at[d], granule.at[d], date_sems.at[d])
        for d in range(dates)
    ]
    for copy in small + large:
        copy.start()
    for copy in small:
        copy.wait()

    own = lax.axis_index("tile")
    side = 1 - 2 * lax.rem(own, 2)
    to_order = (
        lax.broadcasted_iota(jnp.int32, (tile_rows, tile_rows), 1)
        == 2 * lax.rem(lax.broadcasted_iota(jnp.int32, (tile_rows, tile_rows), 0), tile_rows // 2)
        + lax.broadcasted_iota(jnp.int32, (tile_rows, tile_rows), 0) // (tile_rows // 2)
    ).astype(jnp.float32)
    for n, reach in enumerate(reaches):
        wanted = own + side * reach
        slot = jnp.int32(0)
        used = jnp.int32(0)
        for k in range(slots):
            hit = jnp.logical_and(wanted >= 0, targets[0, k] == wanted).astype(jnp.int32)
            slot = slot + k * hit
            used = used + hit
        tap = (
            lax.broadcasted_iota(jnp.int32, (grid_cols, tile_cols), 0)
            - 2 * lax.broadcasted_iota(jnp.int32, (grid_cols, tile_cols), 1)
            - col_offset[0, slot]
        )
        coeffs = coef_x[0, slot].astype(jnp.float32)
        banded = jnp.zeros((grid_cols, tile_cols), jnp.float32)
        for t in range(taps):
            banded = jnp.where(tap == t, coeffs[t : t + 1, :], banded)
        x_mats[n] = banded.astype(jnp.bfloat16)
        tap = (
            lax.broadcasted_iota(jnp.int32, (tile_rows, grid_rows), 1)
            - 2 * lax.broadcasted_iota(jnp.int32, (tile_rows, grid_rows), 0)
            - row_offset[0, slot]
        )
        tap = jnp.where(used > 0, tap, -1)
        coeffs = coef_y[0, slot].astype(jnp.float32)
        banded = jnp.zeros((tile_rows, grid_rows), jnp.float32)
        for t in range(taps):
            banded = jnp.where(tap == t, coeffs[:, t : t + 1], banded)
        ordered = jnp.dot(to_order, banded, preferred_element_type=jnp.float32)
        y_mats[n * tile_rows : (n + 1) * tile_rows] = ordered.astype(jnp.bfloat16)

    half = tile_rows // 2
    for date in range(dates):
        large[date].wait()
        along_y = [
            jnp.dot(y_mats[...], granule[date, b], preferred_element_type=jnp.float32)
            for b in range(bands)
        ]
        for n in range(count):
            rows = jnp.concatenate([part[n * tile_rows : (n + 1) * tile_rows] for part in along_y], 0)
            high = rows.astype(jnp.bfloat16)
            low = (rows - high.astype(jnp.float32)).astype(jnp.bfloat16)
            both = jnp.dot(
                jnp.concatenate([high, low], 0), x_mats[n], preferred_element_type=jnp.float32
            )
            partial = both[: bands * tile_rows] + both[bands * tile_rows :]
            start = 0
            for c, width in enumerate(CHUNKS):
                out = outs[n * len(CHUNKS) + c]
                stride = out.shape[0] // half
                for b in range(width):
                    for parity in range(2):
                        first = (start + b) * tile_rows + parity * half
                        at = date * 2 * width + parity * width + b
                        out[pl.ds(at, half, stride=stride), :] = partial[first : first + half]
                start += width


def resample(reaches, limit, targets, row_offset, col_offset, coef_x, coef_y, granules, after=(), passed_on=()):
    dates, bands, grid_rows, grid_cols = granules.shape
    taps, tile_cols = coef_x.shape[2:]
    tile_rows = coef_y.shape[2]
    count = len(reaches)
    shapes = [
        jax.ShapeDtypeStruct((dates * width * tile_rows, tile_cols), jnp.float32) for width in CHUNKS
    ] * count
    outs = pl.pallas_call(
        functools.partial(resample_kernel, reaches, len(after) + len(passed_on)),
        in_specs=[pl.BlockSpec(memory_space=pltpu.HBM)] * 6
        + [pl.BlockSpec(memory_space=pl.ANY)] * (len(after) + len(passed_on)),
        out_specs=[pl.BlockSpec(memory_space=pltpu.VMEM)] * len(shapes)
        + [pl.BlockSpec(memory_space=pl.ANY)] * len(passed_on),
        out_shape=shapes + [jax.ShapeDtypeStruct(array.shape, array.dtype) for array in passed_on],
        input_output_aliases={6 + len(after) + i: len(shapes) + i for i in range(len(passed_on))},
        scratch_shapes=[
            pltpu.SMEM(targets.shape, jnp.int32),
            pltpu.SMEM(row_offset.shape, jnp.int32),
            pltpu.SMEM(col_offset.shape, jnp.int32),
            pltpu.VMEM(coef_x.shape, coef_x.dtype),
            pltpu.VMEM(coef_y.shape, coef_y.dtype),
            pltpu.VMEM((dates, bands, grid_rows, grid_cols), granules.dtype),
            pltpu.VMEM((count, grid_cols, tile_cols), jnp.bfloat16),
            pltpu.VMEM((count * tile_rows, grid_rows), jnp.bfloat16),
            pltpu.SemaphoreType.DMA((5,)),
            pltpu.SemaphoreType.DMA((dates,)),
        ],
        compiler_params=pltpu.CompilerParams(vmem_limit_bytes=limit),
        cost_estimate=pl.CostEstimate(
            flops=count * dates * bands * tile_rows * grid_cols * (grid_rows + 4 * tile_cols),
            bytes_accessed=granules.size * 2,
            transcendentals=0,
        ),
        name="resample",
    )(targets, row_offset, col_offset, coef_x, coef_y, granules, *after, *passed_on)
    if passed_on:
        return outs
    return [outs[c :: len(CHUNKS)] for c in range(len(CHUNKS))]


def weights_kernel(local_dates, mask, smoother, weights, totals):
    dates = smoother.shape[0]
    masked = smoother[...] * mask[...].astype(jnp.float32)
    me = lax.axis_index("date")
    source = lax.broadcasted_iota(jnp.int32, (dates, dates), 0)
    place = lax.broadcasted_iota(jnp.int32, (dates, dates), 1)
    wanted = ((place // local_dates) ^ me) * local_dates + lax.rem(place, local_dates)
    picks = (source == wanted).astype(jnp.float32)
    weights[...] = jnp.dot(masked, picks, precision=HIGHEST, preferred_element_type=jnp.float32)
    totals[...] = jnp.broadcast_to(jnp.sum(masked, 1, keepdims=True), totals.shape)


def smoothing_weights(local_dates, lanes, mask, smoother):
    return pl.pallas_call(
        functools.partial(weights_kernel, local_dates),
        out_shape=[
            jax.ShapeDtypeStruct(smoother.shape, jnp.float32),
            jax.ShapeDtypeStruct((smoother.shape[0], lanes), jnp.float32),
        ],
        compiler_params=pltpu.CompilerParams(vmem_limit_bytes=LIMIT),
        name="smoothing_weights",
    )(mask, smoother)


def smooth_kernel(pieces, weights, totals, *refs):
    series, out = refs[:-1], refs[-1]
    dates = weights.shape[0]
    stride = out.shape[0] // dates
    held = dates // pieces
    start = 0
    for c, bands in enumerate(CHUNKS):
        for b in range(bands):
            for parity in range(2):
                picked = jnp.concatenate(
                    [
                        part[pl.ds(parity * bands + b, held, stride=2 * bands), :]
                        for part in series[c * pieces : (c + 1) * pieces]
                    ],
                    0,
                )
                total = jnp.dot(
                    weights[...], picked, precision=HIGHEST, preferred_element_type=jnp.float32
                )
                at = 2 * (start + b) + parity
                out[pl.ds(at, dates, stride=stride), :] = total / totals[...]
        start += bands


def smooth(weights, totals, series):
    return pl.pallas_call(
        functools.partial(smooth_kernel, len(series[0])),
        out_shape=jax.ShapeDtypeStruct(
            (sum(part.shape[0] for chunk in series for part in chunk), totals.shape[1]), jnp.float32
        ),
        compiler_params=pltpu.CompilerParams(vmem_limit_bytes=LIMIT),
        name="smooth",
    )(weights, totals, *[part for chunk in series for part in chunk])


def to_pixel_blocks(terms):
    positions = lax.axis_size("date")
    me = lax.axis_index("date")
    core, y = lax.rem(me, 2), me // 2
    terms = [term.reshape(positions // 2, 2, -1, term.shape[-1]) for term in terms]

    def of_core(which):
        picked = [lax.dynamic_index_in_dim(term, which, 1, keepdims=False) for term in terms]
        return picked[0] + picked[1] + picked[2]

    mine, other = of_core(core), of_core(1 - core)
    got = date_swap(other, 1)
    blocks = []
    for distance in range(positions // 2):
        at = y ^ distance
        block = jnp.concatenate(
            [
                lax.dynamic_index_in_dim(mine, at, 0, keepdims=False),
                lax.dynamic_index_in_dim(got, at, 0, keepdims=False),
            ],
            0,
        )
        blocks.append(date_swap(block, 2 * distance) if distance else block)
    return blocks


def body(granules, coef_x, coef_y, row_offset, col_offset, targets, mask, smoother):
    local_dates, bands = granules.shape[:2]
    tile_cols = coef_x.shape[2]
    block_pix = tile_cols * coef_y.shape[2] // lax.axis_size("date")
    coef_x = jnp.transpose(coef_x, (0, 1, 3, 2))

    operands = (targets, row_offset, col_offset, coef_x, coef_y, granules)
    weights, totals = smoothing_weights(local_dates, tile_cols, jnp.transpose(mask), smoother)
    ((far_even, far_odd),) = resample((2, -2), 56 * 1024 * 1024, *operands)
    from_odd = odd_swap(far_odd)
    from_even = even_swap(far_even)
    ((even, odd, own),) = resample((1, -1, 0), LIMIT, *operands)
    arrived_odd = odd_swap(odd + from_even)
    arrived_even = even_swap(even + from_odd)
    blocks = [to_pixel_blocks((own, arrived_odd, arrived_even))]
    smoothed = smooth(weights, totals, blocks)
    return smoothed.reshape(smoother.shape[0], bands, 1, block_pix)


def solution(mesh):
    return jax.shard_map(
        body,
        mesh=mesh,
        in_specs=(
            P("date", None, "tile", None),
            P("tile", None, None, None),
            P("tile", None, None, None),
            P("tile", None),
            P("tile", None),
            P("tile", None),
            P(None, "tile"),
            P(),
        ),
        out_specs=P(None, None, "tile", "date"),
        check_vma=False,
    )
```

```python
import functools

import jax
import jax.numpy as jnp
from jax import lax
from jax.experimental import pallas as pl
from jax.experimental.pallas import tpu as pltpu
from jax.sharding import PartitionSpec as P

HIGHEST = lax.Precision.HIGHEST
LIMIT = 12 * 1024 * 1024


def even_swap(block):
    pairs = [(i, i ^ 1) for i in range(lax.axis_size("tile"))]
    return lax.ppermute(block, "tile", pairs)


def odd_swap(block):
    tiles = lax.axis_size("tile")
    pairs = []
    for date in range(lax.axis_size("date")):
        for tile in range(tiles):
            other, date_to = ((tile - 1) ^ 1) + 1, date
            if tile in (0, tiles - 1):
                other, date_to = tile, date ^ 1
            pairs.append((date * tiles + tile, date_to * tiles + other))
    return lax.ppermute(block, ("date", "tile"), pairs)


def date_swap(block, distance):
    return lax.ppermute(block, "date", [(i, i ^ distance) for i in range(lax.axis_size("date"))])


def resample_kernel(reaches, *refs):
    count = len(reaches)
    inputs, outs, scratch = refs[:6], refs[6 : 6 + count], refs[6 + count :]
    held, (x_mats, y_mats, sems, date_sems) = scratch[:6], scratch[6:]
    targets, row_offset, col_offset, coef_x, coef_y, granule = held
    slots, taps, tile_cols = coef_x.shape[1:]
    tile_rows = coef_y.shape[2]
    dates, bands, grid_rows, grid_cols = granule.shape

    small = [pltpu.make_async_copy(inputs[i], held[i], sems.at[i]) for i in range(5)]
    large = [
        pltpu.make_async_copy(inputs[5].at[d], granule.at[d], date_sems.at[d])
        for d in range(dates)
    ]
    for copy in small + large:
        copy.start()
    for copy in small + large[:2]:
        copy.wait()

    own = lax.axis_index("tile")
    side = 1 - 2 * lax.rem(own, 2)
    to_order = (
        lax.broadcasted_iota(jnp.int32, (tile_rows, tile_rows), 1)
        == 2 * lax.rem(lax.broadcasted_iota(jnp.int32, (tile_rows, tile_rows), 0), tile_rows // 2)
        + lax.broadcasted_iota(jnp.int32, (tile_rows, tile_rows), 0) // (tile_rows // 2)
    ).astype(jnp.float32)
    for n, reach in enumerate(reaches):
        wanted = own + side * reach
        slot = jnp.int32(0)
        used = jnp.int32(0)
        for k in range(slots):
            hit = jnp.logical_and(wanted >= 0, targets[0, k] == wanted).astype(jnp.int32)
            slot = slot + k * hit
            used = used + hit
        coeffs = jnp.pad(coef_x[0, slot].astype(jnp.float32), ((0, 16 - taps), (0, 0)))
        shift = (
            lax.broadcasted_iota(jnp.int32, (8, tile_cols), 0)
            - 2 * lax.broadcasted_iota(jnp.int32, (8, tile_cols), 1)
            - col_offset[0, slot]
        )
        for first in range(0, grid_cols, 16):
            halves = []
            for tap in (shift + first, shift + first + 8):
                place = tap & 7
                picked = jnp.where(
                    tap < 8,
                    jnp.take_along_axis(coeffs[:8], place, axis=0, mode="promise_in_bounds"),
                    jnp.take_along_axis(coeffs[8:], place, axis=0, mode="promise_in_bounds"),
                )
                halves.append(jnp.where((tap & ~15) == 0, picked, 0.0))
            x_mats[n, first : first + 16] = jnp.concatenate(halves, 0).astype(jnp.bfloat16)
        tap = (
            lax.broadcasted_iota(jnp.int32, (tile_rows, grid_rows), 1)
            - 2 * lax.broadcasted_iota(jnp.int32, (tile_rows, grid_rows), 0)
            - row_offset[0, slot]
        )
        tap = jnp.where(used > 0, tap, -1)
        coeffs = coef_y[0, slot].astype(jnp.float32)
        banded = jnp.zeros((tile_rows, grid_rows), jnp.float32)
        for t in range(taps):
            banded = jnp.where(tap == t, coeffs[:, t : t + 1], banded)
        ordered = jnp.dot(to_order, banded, preferred_element_type=jnp.float32)
        y_mats[n * tile_rows : (n + 1) * tile_rows] = ordered.astype(jnp.bfloat16)

    half = tile_rows // 2
    for date in range(dates):
        if date > 0 and date % 2 == 0:
            for copy in large[date : date + 2]:
                copy.wait()
        along_y = [
            jnp.dot(y_mats[...], granule[date, b], preferred_element_type=jnp.float32)
            for b in range(bands)
        ]
        for n in range(count):
            rows = jnp.concatenate([part[n * tile_rows : (n + 1) * tile_rows] for part in along_y], 0)
            high = rows.astype(jnp.bfloat16)
            low = (rows - high.astype(jnp.float32)).astype(jnp.bfloat16)
            partial = jnp.dot(high, x_mats[n], preferred_element_type=jnp.float32) + jnp.dot(
                low, x_mats[n], preferred_element_type=jnp.float32
            )
            stride = 2 * dates * bands
            for b in range(bands):
                for parity in range(2):
                    first = b * tile_rows + parity * half
                    at = date * 2 * bands + parity * bands + b
                    outs[n][pl.ds(at, half, stride=stride), :] = partial[first : first + half]


def resample(reaches, limit, targets, row_offset, col_offset, coef_x, coef_y, granules):
    dates, bands, grid_rows, grid_cols = granules.shape
    tile_cols = coef_x.shape[3]
    tile_rows = coef_y.shape[2]
    count = len(reaches)
    return pl.pallas_call(
        functools.partial(resample_kernel, reaches),
        in_specs=[pl.BlockSpec(memory_space=pltpu.HBM)] * 6,
        out_specs=[pl.BlockSpec(memory_space=pltpu.VMEM)] * count,
        out_shape=[jax.ShapeDtypeStruct((dates * bands * tile_rows, tile_cols), jnp.float32)] * count,
        scratch_shapes=[
            pltpu.SMEM(targets.shape, jnp.int32),
            pltpu.SMEM(row_offset.shape, jnp.int32),
            pltpu.SMEM(col_offset.shape, jnp.int32),
            pltpu.VMEM(coef_x.shape, coef_x.dtype),
            pltpu.VMEM(coef_y.shape, coef_y.dtype),
            pltpu.VMEM(granules.shape, granules.dtype),
            pltpu.VMEM((count, grid_cols, tile_cols), jnp.bfloat16),
            pltpu.VMEM((count * tile_rows, grid_rows), jnp.bfloat16),
            pltpu.SemaphoreType.DMA((5,)),
            pltpu.SemaphoreType.DMA((dates,)),
        ],
        compiler_params=pltpu.CompilerParams(vmem_limit_bytes=limit),
        cost_estimate=pl.CostEstimate(
            flops=count * dates * bands * tile_rows * grid_cols * (grid_rows + 4 * tile_cols),
            bytes_accessed=granules.size * 2,
            transcendentals=0,
        ),
        name="resample",
    )(targets, row_offset, col_offset, coef_x, coef_y, granules)


def weights_kernel(local_dates, mask, smoother, weights):
    dates = smoother.shape[0]
    masked = smoother[...] * mask[...].astype(jnp.float32)
    masked = masked / jnp.sum(masked, 1, keepdims=True)
    me = lax.axis_index("date")
    source = lax.broadcasted_iota(jnp.int32, (dates, dates), 0)
    place = lax.broadcasted_iota(jnp.int32, (dates, dates), 1)
    block = place // local_dates
    wanted = ((block ^ (2 * (block // 4))) ^ me) * local_dates + lax.rem(place, local_dates)
    picks = (source == wanted).astype(jnp.float32)
    ordered = jnp.dot(masked, picks, precision=HIGHEST, preferred_element_type=jnp.float32)
    high = ordered.astype(jnp.bfloat16).astype(jnp.float32)
    weights[...] = jnp.concatenate([high, high, ordered - high], 1)


def smoothing_weights(local_dates, mask, smoother):
    dates = smoother.shape[0]
    return pl.pallas_call(
        functools.partial(weights_kernel, local_dates),
        out_shape=jax.ShapeDtypeStruct((dates, 3 * dates), jnp.float32),
        compiler_params=pltpu.CompilerParams(vmem_limit_bytes=LIMIT),
        name="smoothing_weights",
    )(mask, smoother)


def smooth_kernel(weights, *refs):
    pieces, out = refs[:-1], refs[-1]
    dates, lanes = weights.shape[0], out.shape[1]
    rows = out.shape[0] // dates
    bands, held = rows // 2, dates // len(pieces)
    series = jnp.concatenate(
        [
            jnp.concatenate(
                [piece[pl.ds(parity * bands + b, held, stride=rows), :] for piece in pieces], 0
            )
            for b in range(bands)
            for parity in range(2)
        ],
        1,
    )
    high = series.astype(jnp.bfloat16)
    low = (series - high.astype(jnp.float32)).astype(jnp.bfloat16)
    total = jnp.dot(
        weights[...].astype(jnp.bfloat16),
        jnp.concatenate([high, low, high], 0),
        preferred_element_type=jnp.float32,
    )
    for row in range(rows):
        out[pl.ds(row, dates, stride=rows), :] = total[:, row * lanes : (row + 1) * lanes]


def smooth(weights, pieces):
    return pl.pallas_call(
        smooth_kernel,
        out_shape=jax.ShapeDtypeStruct(
            (sum(piece.shape[0] for piece in pieces), pieces[0].shape[1]), jnp.float32
        ),
        compiler_params=pltpu.CompilerParams(vmem_limit_bytes=LIMIT),
        name="smooth",
    )(weights, *pieces)


def to_pixel_blocks(terms):
    positions = lax.axis_size("date")
    me = lax.axis_index("date")
    core, y = lax.rem(me, 2), me // 2
    terms = [term.reshape(positions // 2, 2, -1, term.shape[-1]) for term in terms]

    def of_core(which):
        picked = [lax.dynamic_index_in_dim(term, which, 1, keepdims=False) for term in terms]
        return picked[0] + picked[1] + picked[2]

    mine, other = of_core(core), of_core(1 - core)
    got = date_swap(other, 1)
    blocks = []
    for distance in [i ^ (i // 2) for i in range(positions // 2)]:
        at = y ^ distance
        block = jnp.concatenate(
            [
                lax.dynamic_index_in_dim(mine, at, 0, keepdims=False),
                lax.dynamic_index_in_dim(got, at, 0, keepdims=False),
            ],
            0,
        )
        blocks.append(date_swap(block, 2 * distance) if distance else block)
    return blocks


def body(granules, coef_x, coef_y, row_offset, col_offset, targets, mask, smoother):
    local_dates, bands = granules.shape[:2]
    tile_cols = coef_x.shape[2]
    block_pix = tile_cols * coef_y.shape[2] // lax.axis_size("date")
    coef_x = jnp.transpose(coef_x, (0, 1, 3, 2))

    operands = (targets, row_offset, col_offset, coef_x, coef_y, granules)
    weights = smoothing_weights(local_dates, jnp.transpose(mask), smoother)
    far_even, far_odd = resample((2, -2), 56 * 1024 * 1024, *operands)
    from_odd = odd_swap(far_odd)
    from_even = even_swap(far_even)
    even, odd, own = resample((1, -1, 0), LIMIT, *operands)
    arrived_odd = odd_swap(odd + from_even)
    arrived_even = even_swap(even + from_odd)
    blocks = to_pixel_blocks((own, arrived_odd, arrived_even))
    smoothed = smooth(weights, blocks)
    return smoothed.reshape(smoother.shape[0], bands, 1, block_pix)


def solution(mesh):
    return jax.shard_map(
        body,
        mesh=mesh,
        in_specs=(
            P("date", None, "tile", None),
            P("tile", None, None, None),
            P("tile", None, None, None),
            P("tile", None),
            P("tile", None),
            P("tile", None),
            P(None, "tile"),
            P(),
        ),
        out_specs=P(None, None, "tile", "date"),
        check_vma=False,
    )
```

```python
import functools

import jax
import jax.numpy as jnp
from jax import lax
from jax.experimental import pallas as pl
from jax.experimental.pallas import tpu as pltpu
from jax.sharding import PartitionSpec as P

HIGHEST = lax.Precision.HIGHEST
LIMIT = 12 * 1024 * 1024


def joint_swap(block, partner, flip):
    tiles = lax.axis_size("tile")
    pairs = []
    for date in range(lax.axis_size("date")):
        for tile in range(tiles):
            to = partner(tile)
            to_date = date ^ flip if 0 <= to < tiles else date ^ 1
            pairs.append((date * tiles + tile, to_date * tiles + (to if 0 <= to < tiles else tile)))
    return lax.ppermute(block, ("date", "tile"), pairs)


def even_swap(block, flip=0):
    return joint_swap(block, lambda tile: tile ^ 1, flip)


def odd_swap(block, flip=0):
    return joint_swap(block, lambda tile: ((tile - 1) ^ 1) + 1, flip)


def date_swap(block, distance):
    return lax.ppermute(block, "date", [(i, i ^ distance) for i in range(lax.axis_size("date"))])


def resample_kernel(reaches, *refs):
    count = len(reaches)
    inputs, outs, scratch = refs[:6], refs[6 : 6 + count], refs[6 + count :]
    held, (x_mats, y_mats, sems, date_sems) = scratch[:6], scratch[6:]
    targets, row_offset, col_offset, coef_x, coef_y, granule = held
    slots, taps, tile_cols = coef_x.shape[1:]
    tile_rows = coef_y.shape[2]
    dates, bands, grid_rows, grid_cols = granule.shape

    small = [pltpu.make_async_copy(inputs[i], held[i], sems.at[i]) for i in range(5)]
    large = [
        pltpu.make_async_copy(inputs[5].at[d], granule.at[d], date_sems.at[d])
        for d in range(dates)
    ]
    for copy in small + large:
        copy.start()
    for copy in small + large[:2]:
        copy.wait()

    own = lax.axis_index("tile")
    side = 1 - 2 * lax.rem(own, 2)
    core = lax.rem(lax.axis_index("date"), 2)
    half = tile_rows // 2
    row = lax.broadcasted_iota(jnp.int32, (tile_rows, tile_rows), 0)
    place = lax.rem(row, half)
    block = 2 * lax.rem(place, half // 2) + (place // (half // 2) ^ core)
    to_order = (
        lax.broadcasted_iota(jnp.int32, (tile_rows, tile_rows), 1) == 2 * block + row // half
    ).astype(jnp.float32)
    for n, reach in enumerate(reaches):
        wanted = own + side * reach
        slot = jnp.int32(0)
        used = jnp.int32(0)
        for k in range(slots):
            hit = jnp.logical_and(wanted >= 0, targets[0, k] == wanted).astype(jnp.int32)
            slot = slot + k * hit
            used = used + hit
        coeffs = jnp.pad(coef_x[0, slot].astype(jnp.float32), ((0, 16 - taps), (0, 0)))
        shift = (
            lax.broadcasted_iota(jnp.int32, (8, tile_cols), 0)
            - 2 * lax.broadcasted_iota(jnp.int32, (8, tile_cols), 1)
            - col_offset[0, slot]
        )
        for first in range(0, grid_cols, 16):
            halves = []
            for tap in (shift + first, shift + first + 8):
                place = tap & 7
                picked = jnp.where(
                    tap < 8,
                    jnp.take_along_axis(coeffs[:8], place, axis=0, mode="promise_in_bounds"),
                    jnp.take_along_axis(coeffs[8:], place, axis=0, mode="promise_in_bounds"),
                )
                halves.append(jnp.where((tap & ~15) == 0, picked, 0.0))
            x_mats[n, first : first + 16] = jnp.concatenate(halves, 0).astype(jnp.bfloat16)
        tap = (
            lax.broadcasted_iota(jnp.int32, (tile_rows, grid_rows), 1)
            - 2 * lax.broadcasted_iota(jnp.int32, (tile_rows, grid_rows), 0)
            - row_offset[0, slot]
        )
        tap = jnp.where(used > 0, tap, -1)
        coeffs = coef_y[0, slot].astype(jnp.float32)
        banded = jnp.zeros((tile_rows, grid_rows), jnp.float32)
        for t in range(taps):
            banded = jnp.where(tap == t, coeffs[:, t : t + 1], banded)
        ordered = jnp.dot(to_order, banded, preferred_element_type=jnp.float32)
        y_mats[n * tile_rows : (n + 1) * tile_rows] = ordered.astype(jnp.bfloat16)

    for date in range(dates):
        if date > 0 and date % 2 == 0:
            for copy in large[date : date + 2]:
                copy.wait()
        along_y = [
            jnp.dot(y_mats[...], granule[date, b], preferred_element_type=jnp.float32)
            for b in range(bands)
        ]
        for n in range(count):
            rows = jnp.concatenate([part[n * tile_rows : (n + 1) * tile_rows] for part in along_y], 0)
            high = rows.astype(jnp.bfloat16)
            low = (rows - high.astype(jnp.float32)).astype(jnp.bfloat16)
            partial = jnp.dot(high, x_mats[n], preferred_element_type=jnp.float32) + jnp.dot(
                low, x_mats[n], preferred_element_type=jnp.float32
            )
            stride = 2 * dates * bands
            for b in range(bands):
                for parity in range(2):
                    first = b * tile_rows + parity * half
                    at = date * 2 * bands + parity * bands + b
                    outs[n][pl.ds(at, half, stride=stride), :] = partial[first : first + half]


def resample(reaches, limit, targets, row_offset, col_offset, coef_x, coef_y, granules):
    dates, bands, grid_rows, grid_cols = granules.shape
    tile_cols = coef_x.shape[3]
    tile_rows = coef_y.shape[2]
    count = len(reaches)
    return pl.pallas_call(
        functools.partial(resample_kernel, reaches),
        in_specs=[pl.BlockSpec(memory_space=pltpu.HBM)] * 6,
        out_specs=[pl.BlockSpec(memory_space=pltpu.VMEM)] * count,
        out_shape=[jax.ShapeDtypeStruct((dates * bands * tile_rows, tile_cols), jnp.float32)] * count,
        scratch_shapes=[
            pltpu.SMEM(targets.shape, jnp.int32),
            pltpu.SMEM(row_offset.shape, jnp.int32),
            pltpu.SMEM(col_offset.shape, jnp.int32),
            pltpu.VMEM(coef_x.shape, coef_x.dtype),
            pltpu.VMEM(coef_y.shape, coef_y.dtype),
            pltpu.VMEM(granules.shape, granules.dtype),
            pltpu.VMEM((count, grid_cols, tile_cols), jnp.bfloat16),
            pltpu.VMEM((count * tile_rows, grid_rows), jnp.bfloat16),
            pltpu.SemaphoreType.DMA((5,)),
            pltpu.SemaphoreType.DMA((dates,)),
        ],
        compiler_params=pltpu.CompilerParams(vmem_limit_bytes=limit),
        cost_estimate=pl.CostEstimate(
            flops=count * dates * bands * tile_rows * grid_cols * (grid_rows + 4 * tile_cols),
            bytes_accessed=granules.size * 2,
            transcendentals=0,
        ),
        name="resample",
    )(targets, row_offset, col_offset, coef_x, coef_y, granules)


def weights_kernel(local_dates, mask, smoother, weights):
    dates = smoother.shape[0]
    masked = smoother[...] * mask[...].astype(jnp.float32)
    masked = masked / jnp.sum(masked, 1, keepdims=True)
    me = lax.axis_index("date")
    source = lax.broadcasted_iota(jnp.int32, (dates, dates), 0)
    place = lax.broadcasted_iota(jnp.int32, (dates, dates), 1)
    block = place // local_dates
    wanted = ((block ^ (2 * (block // 4))) ^ me) * local_dates + lax.rem(place, local_dates)
    picks = (source == wanted).astype(jnp.float32)
    ordered = jnp.dot(masked, picks, precision=HIGHEST, preferred_element_type=jnp.float32)
    high = ordered.astype(jnp.bfloat16).astype(jnp.float32)
    weights[...] = jnp.concatenate([high, high, ordered - high], 1)


def smoothing_weights(local_dates, mask, smoother):
    dates = smoother.shape[0]
    return pl.pallas_call(
        functools.partial(weights_kernel, local_dates),
        out_shape=jax.ShapeDtypeStruct((dates, 3 * dates), jnp.float32),
        compiler_params=pltpu.CompilerParams(vmem_limit_bytes=LIMIT),
        name="smoothing_weights",
    )(mask, smoother)


def smooth_kernel(weights, *refs):
    pieces, out = refs[:-1], refs[-1]
    dates, lanes = weights.shape[0], out.shape[1]
    rows = out.shape[0] // dates
    bands, held = rows // 2, dates // len(pieces)
    series = jnp.concatenate(
        [
            jnp.concatenate(
                [piece[pl.ds(parity * bands + b, held, stride=rows), :] for piece in pieces], 0
            )
            for b in range(bands)
            for parity in range(2)
        ],
        1,
    )
    high = series.astype(jnp.bfloat16)
    low = (series - high.astype(jnp.float32)).astype(jnp.bfloat16)
    total = jnp.dot(
        weights[...].astype(jnp.bfloat16),
        jnp.concatenate([high, low, high], 0),
        preferred_element_type=jnp.float32,
    )
    for row in range(rows):
        out[pl.ds(row, dates, stride=rows), :] = total[:, row * lanes : (row + 1) * lanes]


def smooth(weights, pieces):
    return pl.pallas_call(
        smooth_kernel,
        out_shape=jax.ShapeDtypeStruct(
            (sum(piece.shape[0] for piece in pieces), pieces[0].shape[1]), jnp.float32
        ),
        compiler_params=pltpu.CompilerParams(vmem_limit_bytes=LIMIT),
        name="smooth",
    )(weights, *pieces)


def to_pixel_blocks(mine, got):
    positions = lax.axis_size("date")
    y = lax.axis_index("date") // 2
    mine, got = [part.reshape(positions // 2, -1, part.shape[-1]) for part in (mine, got)]
    blocks = []
    for distance in [i ^ (i // 2) for i in range(positions // 2)]:
        at = y ^ distance
        block = jnp.concatenate(
            [
                lax.dynamic_index_in_dim(mine, at, 0, keepdims=False),
                lax.dynamic_index_in_dim(got, at, 0, keepdims=False),
            ],
            0,
        )
        blocks.append(date_swap(block, 2 * distance) if distance else block)
    return blocks


def body(granules, coef_x, coef_y, row_offset, col_offset, targets, mask, smoother):
    local_dates, bands = granules.shape[:2]
    tile_cols = coef_x.shape[2]
    block_pix = tile_cols * coef_y.shape[2] // lax.axis_size("date")
    coef_x = jnp.transpose(coef_x, (0, 1, 3, 2))

    operands = (targets, row_offset, col_offset, coef_x, coef_y, granules)
    weights = smoothing_weights(local_dates, jnp.transpose(mask), smoother)
    far_even, far_odd = resample((2, -2), 56 * 1024 * 1024, *operands)
    from_odd = odd_swap(far_odd)
    from_even = even_swap(far_even)
    even, odd, own = resample((1, -1, 0), LIMIT, *operands)
    half = own.shape[0] // 2
    mine, other = slice(0, half), slice(half, None)
    odd_mine = odd_swap(odd[mine] + from_even[mine])
    odd_got = odd_swap(odd[other] + from_even[other], 1)
    even_mine = even_swap(even[mine] + from_odd[mine])
    even_got = even_swap(even[other] + from_odd[other], 1)
    own_got = date_swap(own[other], 1)
    blocks = to_pixel_blocks(own[mine] + odd_mine + even_mine, own_got + odd_got + even_got)
    smoothed = smooth(weights, blocks)
    return smoothed.reshape(smoother.shape[0], bands, 1, block_pix)


def solution(mesh):
    return jax.shard_map(
        body,
        mesh=mesh,
        in_specs=(
            P("date", None, "tile", None),
            P("tile", None, None, None),
            P("tile", None, None, None),
            P("tile", None),
            P("tile", None),
            P("tile", None),
            P(None, "tile"),
            P(),
        ),
        out_specs=P(None, None, "tile", "date"),
        check_vma=False,
    )
```

```python
import functools

import jax
import jax.numpy as jnp
from jax import lax
from jax.experimental import pallas as pl
from jax.experimental.pallas import tpu as pltpu
from jax.sharding import PartitionSpec as P

HIGHEST = lax.Precision.HIGHEST
LIMIT = 12 * 1024 * 1024


def joint_swap(block, partner, flip):
    tiles = lax.axis_size("tile")
    pairs = []
    for date in range(lax.axis_size("date")):
        for tile in range(tiles):
            to = partner(tile)
            to_date = date ^ flip if 0 <= to < tiles else date ^ 1
            pairs.append((date * tiles + tile, to_date * tiles + (to if 0 <= to < tiles else tile)))
    return lax.ppermute(block, ("date", "tile"), pairs)


def even_swap(block, flip=0):
    return joint_swap(block, lambda tile: tile ^ 1, flip)


def odd_swap(block, flip=0):
    return joint_swap(block, lambda tile: ((tile - 1) ^ 1) + 1, flip)


def date_swap(block, distance):
    return lax.ppermute(block, "date", [(i, i ^ distance) for i in range(lax.axis_size("date"))])


def resample_kernel(reaches, *refs):
    count = len(reaches)
    inputs, outs, scratch = refs[:6], refs[6 : 6 + count], refs[6 + count :]
    held, (x_mats, y_mats, sems, date_sems) = scratch[:6], scratch[6:]
    targets, row_offset, col_offset, coef_x, coef_y, granule = held
    slots, taps, tile_cols = coef_x.shape[1:]
    tile_rows = coef_y.shape[2]
    dates, bands, grid_rows, grid_cols = granule.shape

    small = [pltpu.make_async_copy(inputs[i], held[i], sems.at[i]) for i in range(5)]
    large = [
        pltpu.make_async_copy(inputs[5].at[d], granule.at[d], date_sems.at[d])
        for d in range(dates)
    ]
    for copy in small + large:
        copy.start()
    for copy in small + large[:2]:
        copy.wait()

    own = lax.axis_index("tile")
    side = 1 - 2 * lax.rem(own, 2)
    core = lax.rem(lax.axis_index("date"), 2)
    half = tile_rows // 2
    row = lax.broadcasted_iota(jnp.int32, (tile_rows, tile_rows), 0)
    place = lax.rem(row, half)
    block = 2 * lax.rem(place, half // 2) + (place // (half // 2) ^ core)
    to_order = (
        lax.broadcasted_iota(jnp.int32, (tile_rows, tile_rows), 1) == 2 * block + row // half
    ).astype(jnp.float32)
    for n, reach in enumerate(reaches):
        wanted = own + side * reach
        slot = jnp.int32(0)
        used = jnp.int32(0)
        for k in range(slots):
            hit = jnp.logical_and(wanted >= 0, targets[0, k] == wanted).astype(jnp.int32)
            slot = slot + k * hit
            used = used + hit
        coeffs = jnp.pad(coef_x[0, slot].astype(jnp.float32), ((0, 16 - taps), (0, 0)))
        shift = (
            lax.broadcasted_iota(jnp.int32, (8, tile_cols), 0)
            - 2 * lax.broadcasted_iota(jnp.int32, (8, tile_cols), 1)
            - col_offset[0, slot]
        )
        for first in range(0, grid_cols, 16):
            halves = []
            for tap in (shift + first, shift + first + 8):
                place = tap & 7
                picked = jnp.where(
                    tap < 8,
                    jnp.take_along_axis(coeffs[:8], place, axis=0, mode="promise_in_bounds"),
                    jnp.take_along_axis(coeffs[8:], place, axis=0, mode="promise_in_bounds"),
                )
                halves.append(jnp.where((tap & ~15) == 0, picked, 0.0))
            x_mats[n, first : first + 16] = jnp.concatenate(halves, 0).astype(jnp.bfloat16)
        tap = (
            lax.broadcasted_iota(jnp.int32, (tile_rows, grid_rows), 1)
            - 2 * lax.broadcasted_iota(jnp.int32, (tile_rows, grid_rows), 0)
            - row_offset[0, slot]
        )
        tap = jnp.where(used > 0, tap, -1)
        coeffs = coef_y[0, slot].astype(jnp.float32)
        banded = jnp.zeros((tile_rows, grid_rows), jnp.float32)
        for t in range(taps):
            banded = jnp.where(tap == t, coeffs[:, t : t + 1], banded)
        ordered = jnp.dot(to_order, banded, preferred_element_type=jnp.float32)
        y_mats[n * tile_rows : (n + 1) * tile_rows] = ordered.astype(jnp.bfloat16)

    for date in range(dates):
        if date > 0 and date % 2 == 0:
            for copy in large[date : date + 2]:
                copy.wait()
        along_y = [
            jnp.dot(y_mats[...], granule[date, b], preferred_element_type=jnp.float32)
            for b in range(bands)
        ]
        for n in range(count):
            rows = jnp.concatenate([part[n * tile_rows : (n + 1) * tile_rows] for part in along_y], 0)
            high = rows.astype(jnp.bfloat16)
            low = (rows - high.astype(jnp.float32)).astype(jnp.bfloat16)
            partial = jnp.dot(
                jnp.concatenate([high, low], 1),
                jnp.concatenate([x_mats[n], x_mats[n]], 0),
                preferred_element_type=jnp.float32,
            )
            stride = 2 * dates * bands
            for b in range(bands):
                for parity in range(2):
                    first = b * tile_rows + parity * half
                    at = date * 2 * bands + parity * bands + b
                    outs[n][pl.ds(at, half, stride=stride), :] = partial[first : first + half]


def resample(reaches, limit, targets, row_offset, col_offset, coef_x, coef_y, granules):
    dates, bands, grid_rows, grid_cols = granules.shape
    tile_cols = coef_x.shape[3]
    tile_rows = coef_y.shape[2]
    count = len(reaches)
    return pl.pallas_call(
        functools.partial(resample_kernel, reaches),
        in_specs=[pl.BlockSpec(memory_space=pltpu.HBM)] * 6,
        out_specs=[pl.BlockSpec(memory_space=pltpu.VMEM)] * count,
        out_shape=[jax.ShapeDtypeStruct((dates * bands * tile_rows, tile_cols), jnp.float32)] * count,
        scratch_shapes=[
            pltpu.SMEM(targets.shape, jnp.int32),
            pltpu.SMEM(row_offset.shape, jnp.int32),
            pltpu.SMEM(col_offset.shape, jnp.int32),
            pltpu.VMEM(coef_x.shape, coef_x.dtype),
            pltpu.VMEM(coef_y.shape, coef_y.dtype),
            pltpu.VMEM(granules.shape, granules.dtype),
            pltpu.VMEM((count, grid_cols, tile_cols), jnp.bfloat16),
            pltpu.VMEM((count * tile_rows, grid_rows), jnp.bfloat16),
            pltpu.SemaphoreType.DMA((5,)),
            pltpu.SemaphoreType.DMA((dates,)),
        ],
        compiler_params=pltpu.CompilerParams(vmem_limit_bytes=limit),
        cost_estimate=pl.CostEstimate(
            flops=count * dates * bands * tile_rows * grid_cols * (grid_rows + 4 * tile_cols),
            bytes_accessed=granules.size * 2,
            transcendentals=0,
        ),
        name="resample",
    )(targets, row_offset, col_offset, coef_x, coef_y, granules)


def weights_kernel(local_dates, mask, smoother, weights):
    dates = smoother.shape[0]
    masked = smoother[...] * mask[...].astype(jnp.float32)
    masked = masked / jnp.sum(masked, 1, keepdims=True)
    me = lax.axis_index("date")
    source = lax.broadcasted_iota(jnp.int32, (dates, dates), 0)
    place = lax.broadcasted_iota(jnp.int32, (dates, dates), 1)
    block = place // local_dates
    wanted = ((block ^ (2 * (block // 4))) ^ me) * local_dates + lax.rem(place, local_dates)
    picks = (source == wanted).astype(jnp.float32)
    ordered = jnp.dot(masked, picks, precision=HIGHEST, preferred_element_type=jnp.float32)
    high = ordered.astype(jnp.bfloat16).astype(jnp.float32)
    weights[...] = jnp.concatenate([high, high, ordered - high], 1)


def smoothing_weights(local_dates, mask, smoother):
    dates = smoother.shape[0]
    return pl.pallas_call(
        functools.partial(weights_kernel, local_dates),
        out_shape=jax.ShapeDtypeStruct((dates, 3 * dates), jnp.float32),
        compiler_params=pltpu.CompilerParams(vmem_limit_bytes=LIMIT),
        name="smoothing_weights",
    )(mask, smoother)


def smooth_kernel(weights, *refs):
    pieces, out = refs[:-1], refs[-1]
    dates, lanes = weights.shape[0], out.shape[1]
    rows = out.shape[0] // dates
    bands, held = rows // 2, dates // len(pieces)
    series = jnp.concatenate(
        [
            jnp.concatenate(
                [piece[pl.ds(parity * bands + b, held, stride=rows), :] for piece in pieces], 0
            )
            for b in range(bands)
            for parity in range(2)
        ],
        1,
    )
    high = series.astype(jnp.bfloat16)
    low = (series - high.astype(jnp.float32)).astype(jnp.bfloat16)
    total = jnp.dot(
        weights[...].astype(jnp.bfloat16),
        jnp.concatenate([high, low, high], 0),
        preferred_element_type=jnp.float32,
    )
    for row in range(rows):
        out[pl.ds(row, dates, stride=rows), :] = total[:, row * lanes : (row + 1) * lanes]


def smooth(weights, pieces):
    return pl.pallas_call(
        smooth_kernel,
        out_shape=jax.ShapeDtypeStruct(
            (sum(piece.shape[0] for piece in pieces), pieces[0].shape[1]), jnp.float32
        ),
        compiler_params=pltpu.CompilerParams(vmem_limit_bytes=LIMIT),
        name="smooth",
    )(weights, *pieces)


def to_pixel_blocks(mine, got):
    positions = lax.axis_size("date")
    y = lax.axis_index("date") // 2
    mine, got = [part.reshape(positions // 2, -1, part.shape[-1]) for part in (mine, got)]
    blocks = []
    for distance in [i ^ (i // 2) for i in range(positions // 2)]:
        at = y ^ distance
        block = jnp.concatenate(
            [
                lax.dynamic_index_in_dim(mine, at, 0, keepdims=False),
                lax.dynamic_index_in_dim(got, at, 0, keepdims=False),
            ],
            0,
        )
        blocks.append(date_swap(block, 2 * distance) if distance else block)
    return blocks


def body(granules, coef_x, coef_y, row_offset, col_offset, targets, mask, smoother):
    local_dates, bands = granules.shape[:2]
    tile_cols = coef_x.shape[2]
    block_pix = tile_cols * coef_y.shape[2] // lax.axis_size("date")
    coef_x = jnp.transpose(coef_x, (0, 1, 3, 2))

    operands = (targets, row_offset, col_offset, coef_x, coef_y, granules)
    weights = smoothing_weights(local_dates, jnp.transpose(mask), smoother)
    far_even, far_odd = resample((2, -2), 56 * 1024 * 1024, *operands)
    from_odd = odd_swap(far_odd)
    from_even = even_swap(far_even)
    even, odd, own = resample((1, -1, 0), LIMIT, *operands)
    half = own.shape[0] // 2
    mine, other = slice(0, half), slice(half, None)
    odd_mine = odd_swap(odd[mine] + from_even[mine])
    odd_got = odd_swap(odd[other] + from_even[other], 1)
    even_mine = even_swap(even[mine] + from_odd[mine])
    even_got = even_swap(even[other] + from_odd[other], 1)
    own_got = date_swap(own[other], 1)
    blocks = to_pixel_blocks(own[mine] + odd_mine + even_mine, own_got + odd_got + even_got)
    smoothed = smooth(weights, blocks)
    return smoothed.reshape(smoother.shape[0], bands, 1, block_pix)


def solution(mesh):
    return jax.shard_map(
        body,
        mesh=mesh,
        in_specs=(
            P("date", None, "tile", None),
            P("tile", None, None, None),
            P("tile", None, None, None),
            P("tile", None),
            P("tile", None),
            P("tile", None),
            P(None, "tile"),
            P(),
        ),
        out_specs=P(None, None, "tile", "date"),
        check_vma=False,
    )
```
